1024 devices in a mesh: expert: 64 (over z_hi, y, core), dp: 16 (over z_lo, x).
Axes of the slice: x: 8, y: 8, z: 8 (z_hi: 4, z_lo: 2; z = z_hi * 2 + z_lo), core: 2. Of those that a mesh axis runs over, the one named last changes fastest.
Arguments:
- dy_values: bfloat16 [16384, 4096], P('expert', 'dp'), may hold values from -6 to 6
- dy_scales: bfloat16 [16384, 32], P('expert', 'dp'), may hold values from 0.25 to 4
- expert_ids: int32 [16384, 1], P('expert'), may hold values from 0 to 63; in each aligned block of 256 rows (0 to 255, 256 to 511, ...) at most 8 rows name the same one
- saved_pre: bfloat16 [32768, 2048], P('expert'), may hold values from -6 to 6
- w_gate: bfloat16 [64, 4096, 1024], P('expert', 'dp'), may hold values from -0.1875 to 0.1875
- w_up: bfloat16 [64, 4096, 1024], P('expert', 'dp'), may hold values from -0.1875 to 0.1875
- w_down: bfloat16 [64, 4096, 1024], P('expert', 'dp'), may hold values from -0.09375 to 0.09375
Outputs:
- grad_input: bfloat16 [16384, 4096], P('expert', 'dp')
- grad_down: float32 [64, 4096, 1024], P('expert', 'dp')
The draws below stay inside these ranges and needn't reach their ends.
Inputs may be any that keep to these rules, and one draw needn't show every extreme that they name: `expert_ids`: among the rows of one index of expert (aligned blocks of 256 rows) no expert occurs more than 8 times.
All inputs are finite; a program needn't handle non-finite values.
Results may differ from the reference program's by a relative error of at most 0.0057.
Values may be sent and summed in bfloat16 or wider, within the bound.
A program may use at most 32 MiB of HBM per device.

```python
import math
import jax
import jax.numpy as jnp
import numpy as np
from jax import lax

D = 4096
FF = 1024
BLOCK = 128
ROWS_DEV = 256
SLOTS = 512
EXPERTS = 64
CAP = 8
ROWS = 16384
SLOT_ROWS = 32768


def steps_of(rng, dims, shards, smallest, high):
    loudness, own = 1.0, jax.random.fold_in(rng, 6)
    for dim, blocks in shards:
        draws = jnp.exp(jax.random.uniform(jax.random.fold_in(own, dim), (blocks,), jnp.float32, smallest / len(shards), high / len(shards)))
        loudness = loudness * jnp.repeat(draws, dims[dim] // blocks).reshape([-1 if axis == dim else 1 for axis in range(len(dims))])
    return loudness


def routed_block(key, own, number, rows, amount, top, limit, lean):
    sequence = jax.random.permutation(key, amount)
    packed, ordinary = shares(amount, rows * top, limit, lean, True), shares(amount, rows * top, limit, lean, False)
    places = jnp.arange(amount)

    def named(tallies, offset_by):
        used = int((tallies > 0).sum())
        fixed = max(1, used // 4)
        shifted = fixed + (places - fixed + offset_by * (used - fixed)) % max(1, amount - fixed)
        return jnp.zeros((amount,), jnp.int32).at[sequence[jnp.where(places < fixed, places, shifted)]].set(jnp.asarray(tallies, jnp.int32))

    tallies = jnp.where(number % 4 == 0, named(packed, number // 4), named(ordinary, number - number // 4 - 1))
    mixed = jax.random.permutation(jax.random.fold_in(own, 3), amount)
    source_of, receiver = mixed[0:amount // 2 * 2:2], mixed[1:amount // 2 * 2:2]
    margin = jnp.minimum(tallies[source_of] - 1, limit - tallies[receiver]) // 2
    margin = jnp.where((source_of == sequence[0]) | (receiver == sequence[0]) | (tallies[receiver] == 0), 0, jnp.maximum(margin, 0))
    shifted = jax.random.randint(jax.random.fold_in(own, 4), (amount // 2,), 0, 1 << 20) % (margin + 1)
    tallies = tallies.at[source_of].add(-shifted).at[receiver].add(shifted)
    items = jnp.searchsorted(jnp.cumsum(tallies), jnp.arange(rows * top), side="right").astype(jnp.int32)
    table = items.reshape(top, rows).T
    table = table[jax.random.permutation(jax.random.fold_in(own, 1), rows)]
    offset_by = jax.random.randint(jax.random.fold_in(own, 2), (rows, 1), 0, top)
    return jnp.take_along_axis(table, (jnp.arange(top)[None, :] + offset_by) % top, axis=1)


def shares(number_of, total, reach, slope, full):
    weights = [(1 << 20) // math.isqrt(standing ** slope) + 1 for standing in range(1, number_of + 1)]
    largest = reach if full else min(reach, max(-(-total // number_of), total * weights[0] // sum(weights)))
    least = 1 if total - largest >= number_of - 1 else 0
    holding, surplus = [largest] + [least] * (number_of - 1), total - largest - least * (number_of - 1)
    while surplus > 0:
        movable = [i for i in range(1, number_of) if holding[i] < largest] or [i for i in range(1, number_of) if holding[i] < reach]
        mass, budget = sum([weights[i] for i in movable]), surplus
        for i in movable:
            extra = min(reach - holding[i], max(1, budget * weights[i] // mass), surplus)
            holding[i] = holding[i] + extra
            surplus = surplus - extra
    return np.array(holding)


def scatter_about(rng, shape, scale, limit, pieces=(), held_as=jnp.bfloat16):
    result = jax.random.normal(rng, shape, jnp.float32) * scale
    if len(pieces) > 0:
        result = steps_of(rng, shape, pieces, -0.22, 0.18) * result
    return jnp.clip(result, min=-limit, max=limit).astype(held_as)


def setup_inputs(seed: int = 0) -> dict:
    seeds = jax.random.split(jax.random.key(seed), 8)
    dy_values = scatter_about(seeds[0], (ROWS, D), 1.0, 6.0, ((0, 64), (1, 16)))
    dy_scales = jnp.clip(jnp.exp(math.log(4.0) - 2.7725887 * jax.random.uniform(seeds[1], (ROWS, D // BLOCK), jnp.float32) ** steps_of(seeds[1], (ROWS, D // BLOCK), ((0, 64), (1, 16)), -0.2, 0.2)), 0.25, 4.0).astype(jnp.bfloat16)
    expert_ids_keys = jax.random.split(jax.random.fold_in(seeds[2], 1), ROWS // ROWS_DEV)
    expert_ids_turns = jax.random.permutation(jax.random.fold_in(seeds[2], 3), ROWS // ROWS_DEV)
    expert_ids = jax.vmap(lambda own, number: routed_block(jax.random.fold_in(seeds[2], 2), own, number, ROWS_DEV, EXPERTS, 1, CAP, 2))(expert_ids_keys, expert_ids_turns).reshape((ROWS, 1))
    saved_pre = scatter_about(seeds[3], (SLOT_ROWS, 2 * FF), 1.0, 6.0, ((0, 64),))
    w_gate = scatter_about(seeds[4], (EXPERTS, D, FF), FF ** -0.5, 0.1875, ((0, 64), (1, 16)))
    w_up = scatter_about(seeds[5], (EXPERTS, D, FF), FF ** -0.5, 0.1875, ((0, 64), (1, 16)))
    w_down = scatter_about(seeds[6], (EXPERTS, D, FF), D ** -0.5, 0.09375, ((0, 64), (1, 16)))
    return {"dy_values": dy_values, "dy_scales": dy_scales, "expert_ids": expert_ids, "saved_pre": saved_pre, "w_gate": w_gate, "w_up": w_up, "w_down": w_down}


def dequantize(values, scales):
    row_count, feature_count = values.shape
    block_count = scales.shape[1]
    blocked = values.astype(jnp.float32).reshape(row_count, block_count, feature_count // block_count)
    blocked = blocked * scales.astype(jnp.float32)[:, :, None]
    return blocked.reshape(row_count, feature_count).astype(jnp.bfloat16)


def swiglu_back(hidden_grad, gate_pre, up_pre):
    sigmoid_gate = jax.nn.sigmoid(gate_pre)
    d_gate = hidden_grad * up_pre * sigmoid_gate * (1.0 + gate_pre * (1.0 - sigmoid_gate))
    d_up = hidden_grad * jax.nn.silu(gate_pre)
    return jnp.concatenate([d_gate, d_up], axis=1).astype(jnp.bfloat16)


def reference(dy_values, dy_scales, expert_ids, saved_pre, w_gate, w_up, w_down):
    row_total = dy_values.shape[0]
    route_ids = expert_ids[:, 0].astype(jnp.int32)
    per_expert = SLOTS // EXPERTS
    by_source = route_ids.reshape(-1, ROWS_DEV)
    onehot = (by_source[:, :, None] == jnp.arange(EXPERTS, dtype=jnp.int32)[None, None, :]).astype(jnp.int32)
    earlier = jnp.cumsum(onehot, axis=1) - onehot
    rank = jnp.sum(earlier * onehot, axis=2).reshape(-1)
    source = jnp.arange(row_total, dtype=jnp.int32) // ROWS_DEV
    position = (route_ids * SLOTS + source * per_expert + rank).astype(jnp.int32)
    grad_rows = dequantize(dy_values, dy_scales)
    owner = jnp.full((SLOT_ROWS,), row_total, jnp.int32).at[position].set(jnp.arange(row_total, dtype=jnp.int32))
    padded_rows = jnp.concatenate([grad_rows, jnp.zeros((1, D), jnp.bfloat16)], axis=0)

    def one_expert(expert):
        first = (expert * SLOTS).astype(jnp.int32)
        members = lax.dynamic_slice_in_dim(owner, first, SLOTS)
        received = padded_rows[members]
        saved = lax.dynamic_slice_in_dim(saved_pre, first, SLOTS, 0)
        gate_pre = saved[:, :FF].astype(jnp.float32)
        up_pre = saved[:, FF:].astype(jnp.float32)
        hidden = (jax.nn.silu(gate_pre) * up_pre).astype(jnp.bfloat16)
        hidden_grad = jnp.dot(received, w_down[expert], preferred_element_type=jnp.float32)
        pre_grad = swiglu_back(hidden_grad, gate_pre, up_pre)
        paired = jnp.concatenate([w_gate[expert], w_up[expert]], axis=1)
        slot_grad = lax.dot_general(pre_grad, paired, (((1,), (1,)), ((), ())), preferred_element_type=jnp.float32).astype(jnp.bfloat16)
        weight_grad = lax.dot_general(received, hidden, (((0,), (0,)), ((), ())), preferred_element_type=jnp.float32)
        return weight_grad, slot_grad

    grad_down, slot_grads = lax.map(one_expert, jnp.arange(EXPERTS, dtype=jnp.int32))
    grad_input = slot_grads.reshape(SLOT_ROWS, D)[position]
    return grad_input, grad_down
```

```python
import jax
import jax.numpy as jnp
from jax import lax
from jax.experimental import pallas as pl
from jax.experimental.pallas import tpu as pltpu
from jax.sharding import PartitionSpec as P

MESH = pl.DeviceIdType.MESH
F32, BF16 = jnp.float32, jnp.bfloat16

RING = 8
CAP = 8

REDUCE_RIGHT = ((0, 4), (1, 3), (0, 3), (1, 2), (0, 2), (1, 1), (0, 1))
REDUCE_LEFT = ((1, 4), (0, 3), (1, 3), (0, 2), (1, 2), (0, 1), (1, 1))
GATHER_RIGHT = ((0, 1), (1, 1), (0, 2), (1, 2), (0, 3), (1, 3), (0, 4))
GATHER_LEFT = ((1, 1), (0, 1), (1, 2), (0, 2), (1, 3), (0, 3), (1, 4))


def kernel(
    ids_ref,
    dy_ref,
    scale_ref,
    saved_hbm,
    gate_hbm,
    up_hbm,
    down_hbm,
    gi_out,
    gd_out,
    saved,
    w_gate,
    w_up,
    w_down,
    pick,
    send,
    recv,
    received,
    hidden,
    c_gate,
    c_up,
    part,
    rs_send,
    rs_recv,
    acc,
    z_send,
    z_recv,
    grads,
    back_send,
    back_recv,
    gd,
    gi,
    in_sem,
    out_sem,
    a2a_sem,
    rs_ssem,
    rs_rsem,
    z_sem,
    ag_ssem,
    ag_rsem,
    back_sem,
):
    experts = send.shape[0]
    slots, feats = received.shape
    ff = hidden.shape[1]
    half_ff = ff // 2
    chunk = slots // RING
    per_chunk = chunk // CAP
    rows = dy_ref.shape[0]

    me = lax.axis_index("expert")
    dp = lax.axis_index("dp")
    x = lax.rem(dp, RING)
    base = dp - x
    right = base + lax.rem(x + 1, RING)
    left = base + lax.rem(x + RING - 1, RING)
    other = lax.rem(dp + RING, 2 * RING)

    loads = [
        pltpu.make_async_copy(src, dst, in_sem.at[k])
        for k, (src, dst) in enumerate(
            ((saved_hbm, saved), (down_hbm, w_down), (gate_hbm, w_gate), (up_hbm, w_up))
        )
    ]
    for load in loads:
        load.start()

    barrier = pltpu.get_barrier_semaphore()

    def greet(i, carry):
        pl.semaphore_signal(
            barrier, inc=1, device_id={"expert": lax.rem(me + i, experts)}, device_id_type=MESH
        )
        return carry

    lax.fori_loop(1, experts, greet, 0)
    for peer in (right, left, other):
        pl.semaphore_signal(barrier, inc=1, device_id={"dp": peer}, device_id_type=MESH)

    ids = ids_ref[...]
    named = jnp.where(lax.broadcasted_iota(jnp.int32, (experts, rows), 0) == ids, 1.0, 0.0)
    before = jnp.where(
        lax.broadcasted_iota(jnp.int32, (rows, rows), 0)
        < lax.broadcasted_iota(jnp.int32, (rows, rows), 1),
        1.0,
        0.0,
    ).astype(BF16)
    earlier = jnp.dot(named.astype(BF16), before, preferred_element_type=F32)
    rank = jnp.sum(earlier * named, axis=0, keepdims=True)
    position = ids * CAP + rank.astype(jnp.int32)
    hit = lax.broadcasted_iota(jnp.int32, (slots, rows), 0) == position
    pick[...] = jnp.where(hit, 1.0, 0.0).astype(BF16)
    halves = []
    for h in range(2):
        scaled = jnp.where(hit, scale_ref[h : h + 1, :].astype(F32), 0.0).astype(BF16)
        rows_h = jnp.dot(
            scaled, dy_ref[:, h * 128 : (h + 1) * 128], preferred_element_type=F32
        )
        halves.append(rows_h.reshape(experts, CAP, 128))
    send[...] = jnp.concatenate(halves, axis=1).astype(BF16)

    pl.semaphore_wait(barrier, experts - 1 + 3)

    def dispatch(i, carry):
        to = lax.rem(me + i, experts)
        pltpu.make_async_remote_copy(
            src_ref=send.at[to],
            dst_ref=recv.at[me],
            send_sem=a2a_sem.at[0],
            recv_sem=a2a_sem.at[1],
            device_id={"expert": to},
            device_id_type=MESH,
        ).start()
        return carry

    lax.fori_loop(1, experts, dispatch, 0)
    recv[pl.ds(me, 1)] = send[pl.ds(me, 1)]

    loads[0].wait()
    step = 16

    def activate(i, carry):
        at = pl.ds(pl.multiple_of(i * step, step), step)
        gate = saved[at, :ff].astype(F32)
        up = saved[at, ff:].astype(F32)
        sig = jax.nn.sigmoid(gate)
        silu = gate * sig
        c_up[at, :] = silu
        c_gate[at, :] = up * sig * (1.0 + gate * (1.0 - sig))
        hidden[at, :] = (silu * up).astype(BF16)
        return carry

    lax.fori_loop(0, slots // step, activate, 0)

    def all_but_one(buf_a, buf_b, sems):
        n = pl.ds(0, experts - 1)
        return pltpu.make_async_remote_copy(
            src_ref=buf_a.at[n],
            dst_ref=buf_b.at[n],
            send_sem=sems.at[0],
            recv_sem=sems.at[1],
            device_id={"expert": lax.rem(me + 1, experts)},
            device_id_type=MESH,
        )

    arrived = all_but_one(send, recv, a2a_sem)
    arrived.wait_recv()
    got = recv[...].astype(F32)
    received[...] = jnp.concatenate(
        [got[:, :CAP].reshape(slots, 128), got[:, CAP:].reshape(slots, 128)], axis=1
    ).astype(BF16)

    loads[1].wait()
    block = 128

    def project(i, carry):
        at = pl.ds(pl.multiple_of(i * block, block), block)
        part[at, :] = jnp.dot(received[at, :], w_down[...], preferred_element_type=F32)
        return carry

    lax.fori_loop(0, slots // block, project, 0)

    def own(c, h):
        at = pl.ds(pl.multiple_of(c * chunk, chunk), chunk)
        return part[at, h * half_ff : (h + 1) * half_ff]

    sides = ((right, REDUCE_RIGHT, 1), (left, REDUCE_LEFT, RING - 1))

    def rs_copy(side, k):
        return pltpu.make_async_remote_copy(
            src_ref=rs_send.at[side, k],
            dst_ref=rs_recv.at[side, k],
            send_sem=rs_ssem.at[side, k],
            recv_sem=rs_rsem.at[side, k],
            device_id={"dp": sides[side][0]},
            device_id_type=MESH,
        )

    for k in range(7):
        for side in range(2):
            h, hops = sides[side][1][k]
            c = lax.rem(x + hops * sides[side][2], RING)
            value = own(c, h)
            if k >= 2:
                rs_copy(side, k - 2).wait_recv()
                value = value + rs_recv[side, k - 2].astype(F32)
            rs_send[side, k] = value.astype(BF16)
            rs_copy(side, k).start()
        if k == 1:

            def weight_grad(i, carry):
                at = pl.ds(pl.multiple_of(i * 256, 256), 256)
                gd[:, at] = lax.dot_general(
                    received[...],
                    hidden[:, at],
                    (((0,), (0,)), ((), ())),
                    preferred_element_type=F32,
                )
                return carry

            lax.fori_loop(0, ff // 256, weight_grad, 0)
            gd_copy = pltpu.make_async_copy(gd, gd_out, out_sem.at[0])
            gd_copy.start()

    def z_copy(h):
        return pltpu.make_async_remote_copy(
            src_ref=z_send.at[h],
            dst_ref=z_recv.at[h],
            send_sem=z_sem.at[0, h],
            recv_sem=z_sem.at[1, h],
            device_id={"dp": other},
            device_id_type=MESH,
        )

    for h in (1, 0):
        total = own(x, h)
        for side in range(2):
            k = sides[side][1].index((h, 1))
            rs_copy(side, k).wait_recv()
            total = total + rs_recv[side, k].astype(F32)
        acc[h] = total
        z_send[h] = total.astype(BF16)
        z_copy(h).start()

    ways = ((right, GATHER_RIGHT, RING - 1), (left, GATHER_LEFT, 1))

    def ag_copy(side, h, hops):
        k = ways[side][1].index((h, hops))
        c = lax.rem(x + (hops - 1) * ways[side][2], RING)
        return pltpu.make_async_remote_copy(
            src_ref=grads.at[c, h],
            dst_ref=grads.at[c, h],
            send_sem=ag_ssem.at[side, k],
            recv_sem=ag_rsem.at[side, k],
            device_id={"dp": ways[side][0]},
            device_id_type=MESH,
        )

    for h in (1, 0):
        z_copy(h).wait_recv()
        grads[x, h] = (acc[h] + z_recv[h].astype(F32)).astype(BF16)
        for side in range(2):
            ag_copy(side, h, 1).start()

    loads[2].wait()
    loads[3].wait()

    def finish(chunks):
        d_gate, d_up = [], []
        for c in chunks:
            at = pl.ds(pl.multiple_of(c * chunk, chunk), chunk)
            g = jnp.concatenate([grads[c, 0], grads[c, 1]], axis=1).astype(F32)
            d_gate.append((g * c_gate[at, :]).astype(BF16))
            d_up.append((g * c_up[at, :]).astype(BF16))
        if len(chunks) > 1:
            d_gate, d_up = [jnp.concatenate(d_gate, axis=0)], [jnp.concatenate(d_up, axis=0)]
        across = (((1,), (1,)), ((), ()))
        out = lax.dot_general(d_gate[0], w_gate[...], across, preferred_element_type=F32)
        out = out + lax.dot_general(d_up[0], w_up[...], across, preferred_element_type=F32)
        for n, c in enumerate(chunks):
            mine = out[n * chunk : (n + 1) * chunk]
            first = c * per_chunk
            back_send[pl.ds(first, per_chunk)] = jnp.concatenate(
                [
                    mine[:, :128].reshape(per_chunk, CAP, 128),
                    mine[:, 128:].reshape(per_chunk, CAP, 128),
                ],
                axis=1,
            ).astype(BF16)

            def give_back(i, carry):
                to = first + i

                @pl.when(to != me)
                def _():
                    pltpu.make_async_remote_copy(
                        src_ref=back_send.at[to],
                        dst_ref=back_recv.at[me],
                        send_sem=back_sem.at[0],
                        recv_sem=back_sem.at[1],
                        device_id={"expert": to},
                        device_id_type=MESH,
                    ).start()

                return carry

            lax.fori_loop(0, per_chunk, give_back, 0)

    finish([x])
    for hops in range(1, RING // 2 + 1):
        for n in range(2):
            for side in range(2):
                h = n if side == 0 else 1 - n
                if (h, hops) in ways[side][1]:
                    ag_copy(side, h, hops).wait_recv()
                    if (h, hops + 1) in ways[side][1]:
                        ag_copy(side, h, hops + 1).start()
        if hops < RING // 2:
            finish([lax.rem(x + RING - hops, RING), lax.rem(x + hops, RING)])
        else:
            finish([lax.rem(x + hops, RING)])

    back_recv[pl.ds(me, 1)] = back_send[pl.ds(me, 1)]
    returned = all_but_one(back_send, back_recv, back_sem)
    returned.wait_recv()
    got = back_recv[...].astype(F32)
    table = jnp.concatenate(
        [got[:, :CAP].reshape(slots, 128), got[:, CAP:].reshape(slots, 128)], axis=1
    ).astype(BF16)
    gi[...] = lax.dot_general(
        pick[...], table, (((0,), (0,)), ((), ())), preferred_element_type=F32
    ).astype(BF16)
    gi_copy = pltpu.make_async_copy(gi, gi_out, out_sem.at[1])
    gi_copy.start()

    arrived.wait_send()
    returned.wait_send()
    for side in range(2):
        for k in range(7):
            rs_copy(side, k).wait_send()
        for h, hops in ways[side][1]:
            ag_copy(side, h, hops).wait_send()
    for h in range(2):
        z_copy(h).wait_send()
    gd_copy.wait()
    gi_copy.wait()


def per_device(dy_values, dy_scales, expert_ids, saved_pre, w_gate, w_up, w_down):
    rows, feats = dy_values.shape
    slots = saved_pre.shape[0]
    ff = w_down.shape[2]
    experts = slots // CAP
    chunk = slots // RING
    vmem = pl.BlockSpec(memory_space=pltpu.VMEM)
    anywhere = pl.BlockSpec(memory_space=pl.ANY)
    grad_input, grad_down = pl.pallas_call(
        kernel,
        out_shape=(
            jax.ShapeDtypeStruct((rows, feats), BF16),
            jax.ShapeDtypeStruct((feats, ff), F32),
        ),
        in_specs=[vmem] * 3 + [anywhere] * 4,
        out_specs=(anywhere, anywhere),
        scratch_shapes=[
            pltpu.VMEM((slots, 2 * ff), BF16),
            pltpu.VMEM((feats, ff), BF16),
            pltpu.VMEM((feats, ff), BF16),
            pltpu.VMEM((feats, ff), BF16),
            pltpu.VMEM((slots, rows), BF16),
            pltpu.VMEM((experts, 2 * CAP, 128), BF16),
            pltpu.VMEM((experts, 2 * CAP, 128), BF16),
            pltpu.VMEM((slots, feats), BF16),
            pltpu.VMEM((slots, ff), BF16),
            pltpu.VMEM((slots, ff), F32),
            pltpu.VMEM((slots, ff), F32),
            pltpu.VMEM((slots, ff), F32),
            pltpu.VMEM((2, 7, chunk, ff // 2), BF16),
            pltpu.VMEM((2, 7, chunk, ff // 2), BF16),
            pltpu.VMEM((2, chunk, ff // 2), F32),
            pltpu.VMEM((2, chunk, ff // 2), BF16),
            pltpu.VMEM((2, chunk, ff // 2), BF16),
            pltpu.VMEM((RING, 2, chunk, ff // 2), BF16),
            pltpu.VMEM((experts, 2 * CAP, 128), BF16),
            pltpu.VMEM((experts, 2 * CAP, 128), BF16),
            pltpu.VMEM((feats, ff), F32),
            pltpu.VMEM((rows, feats), BF16),
            pltpu.SemaphoreType.DMA((4,)),
            pltpu.SemaphoreType.DMA((2,)),
            pltpu.SemaphoreType.DMA((2,)),
            pltpu.SemaphoreType.DMA((2, 7)),
            pltpu.SemaphoreType.DMA((2, 7)),
            pltpu.SemaphoreType.DMA((2, 2)),
            pltpu.SemaphoreType.DMA((2, 7)),
            pltpu.SemaphoreType.DMA((2, 7)),
            pltpu.SemaphoreType.DMA((2,)),
        ],
        compiler_params=pltpu.CompilerParams(
            collective_id=0, has_side_effects=True, vmem_limit_bytes=60 * 1024 * 1024
        ),
        name="experts_backward",
    )(
        expert_ids.reshape(1, rows),
        dy_values,
        dy_scales.T,
        saved_pre,
        w_gate[0],
        w_up[0],
        w_down[0],
    )
    return grad_input, grad_down[None]


def solution(mesh):
    return jax.shard_map(
        per_device,
        mesh=mesh,
        in_specs=(
            P("expert", "dp"),
            P("expert", "dp"),
            P("expert", None),
            P("expert", None),
            P("expert", "dp", None),
            P("expert", "dp", None),
            P("expert", "dp", None),
        ),
        out_specs=(P("expert", "dp"), P("expert", "dp", None)),
        check_vma=False,
    )
```

```python
import jax
import jax.numpy as jnp
from jax import lax
from jax.experimental import pallas as pl
from jax.experimental.pallas import tpu as pltpu
from jax.sharding import PartitionSpec as P

MESH = pl.DeviceIdType.MESH
F32, BF16 = jnp.float32, jnp.bfloat16

RING = 8
CAP = 8

REDUCE_RIGHT = ((0, 4), (1, 3), (0, 3), (1, 2), (0, 2), (1, 1), (0, 1))
REDUCE_LEFT = ((1, 4), (0, 3), (1, 3), (0, 2), (1, 2), (0, 1), (1, 1))
GATHER_RIGHT = ((0, 1), (1, 1), (0, 2), (1, 2), (0, 3), (1, 3), (0, 4))
GATHER_LEFT = ((1, 1), (0, 1), (1, 2), (0, 2), (1, 3), (0, 3), (1, 4))


def kernel(
    ids_ref,
    dy_ref,
    scale_ref,
    saved_hbm,
    gate_hbm,
    up_hbm,
    down_hbm,
    gi,
    gd,
    saved,
    w_gate,
    w_up,
    w_down,
    pick,
    send,
    recv,
    received,
    hidden,
    c_gate,
    c_up,
    part,
    rs_send,
    rs_recv,
    acc,
    z_send,
    z_recv,
    grads,
    back_send,
    back_recv,
    in_sem,
    a2a_sem,
    rs_ssem,
    rs_rsem,
    z_sem,
    ag_ssem,
    ag_rsem,
    back_sem,
):
    experts = send.shape[0]
    slots, feats = received.shape
    ff = hidden.shape[1]
    half_ff = ff // 2
    chunk = slots // RING
    per_chunk = chunk // CAP
    rows = dy_ref.shape[0]

    me = lax.axis_index("expert")
    dp = lax.axis_index("dp")
    x = lax.rem(dp, RING)
    base = dp - x
    right = base + lax.rem(x + 1, RING)
    left = base + lax.rem(x + RING - 1, RING)
    other = lax.rem(dp + RING, 2 * RING)

    loads = [
        pltpu.make_async_copy(src, dst, in_sem.at[k])
        for k, (src, dst) in enumerate(
            ((saved_hbm, saved), (down_hbm, w_down), (gate_hbm, w_gate), (up_hbm, w_up))
        )
    ]
    for load in loads:
        load.start()

    barrier = pltpu.get_barrier_semaphore()

    def greet(i, carry):
        pl.semaphore_signal(
            barrier, inc=1, device_id={"expert": lax.rem(me + i, experts)}, device_id_type=MESH
        )
        return carry

    lax.fori_loop(1, experts, greet, 0)
    for peer in (right, left, other):
        pl.semaphore_signal(barrier, inc=1, device_id={"dp": peer}, device_id_type=MESH)

    ids = ids_ref[...]
    named = jnp.where(lax.broadcasted_iota(jnp.int32, (experts, rows), 0) == ids, 1.0, 0.0)
    before = jnp.where(
        lax.broadcasted_iota(jnp.int32, (rows, rows), 0)
        < lax.broadcasted_iota(jnp.int32, (rows, rows), 1),
        1.0,
        0.0,
    ).astype(BF16)
    earlier = jnp.dot(named.astype(BF16), before, preferred_element_type=F32)
    rank = jnp.sum(earlier * named, axis=0, keepdims=True)
    position = ids * CAP + rank.astype(jnp.int32)
    hit = lax.broadcasted_iota(jnp.int32, (slots, rows), 0) == position
    pick[...] = jnp.where(hit, 1.0, 0.0).astype(BF16)
    halves = []
    for h in range(2):
        scaled = jnp.where(hit, scale_ref[h : h + 1, :].astype(F32), 0.0).astype(BF16)
        rows_h = jnp.dot(
            scaled, dy_ref[:, h * 128 : (h + 1) * 128], preferred_element_type=F32
        )
        halves.append(rows_h.reshape(experts, CAP, 128))
    send[...] = jnp.concatenate(halves, axis=1).astype(BF16)

    pl.semaphore_wait(barrier, experts - 1 + 3)

    def dispatch(i, carry):
        to = lax.rem(me + i, experts)
        pltpu.make_async_remote_copy(
            src_ref=send.at[to],
            dst_ref=recv.at[me],
            send_sem=a2a_sem.at[0],
            recv_sem=a2a_sem.at[1],
            device_id={"expert": to},
            device_id_type=MESH,
        ).start()
        return carry

    lax.fori_loop(1, experts, dispatch, 0)
    recv[pl.ds(me, 1)] = send[pl.ds(me, 1)]

    loads[0].wait()
    step = 16

    def activate(i, carry):
        at = pl.ds(pl.multiple_of(i * step, step), step)
        gate = saved[at, :ff].astype(F32)
        up = saved[at, ff:].astype(F32)
        sig = jax.nn.sigmoid(gate)
        silu = gate * sig
        c_up[at, :] = silu
        c_gate[at, :] = up * sig * (1.0 + gate * (1.0 - sig))
        hidden[at, :] = (silu * up).astype(BF16)
        return carry

    lax.fori_loop(0, slots // step, activate, 0)

    def all_but_one(buf_a, buf_b, sems):
        n = pl.ds(0, experts - 1)
        return pltpu.make_async_remote_copy(
            src_ref=buf_a.at[n],
            dst_ref=buf_b.at[n],
            send_sem=sems.at[0],
            recv_sem=sems.at[1],
            device_id={"expert": lax.rem(me + 1, experts)},
            device_id_type=MESH,
        )

    arrived = all_but_one(send, recv, a2a_sem)
    arrived.wait_recv()
    got = recv[...].astype(F32)
    received[...] = jnp.concatenate(
        [got[:, :CAP].reshape(slots, 128), got[:, CAP:].reshape(slots, 128)], axis=1
    ).astype(BF16)

    loads[1].wait()
    block = 128

    def project(i, carry):
        at = pl.ds(pl.multiple_of(i * block, block), block)
        part[at, :] = jnp.dot(received[at, :], w_down[...], preferred_element_type=F32)
        return carry

    lax.fori_loop(0, slots // block, project, 0)

    def own(c, h):
        at = pl.ds(pl.multiple_of(c * chunk, chunk), chunk)
        return part[at, h * half_ff : (h + 1) * half_ff]

    sides = ((right, REDUCE_RIGHT, 1), (left, REDUCE_LEFT, RING - 1))

    def rs_copy(side, k):
        return pltpu.make_async_remote_copy(
            src_ref=rs_send.at[side, k],
            dst_ref=rs_recv.at[side, k],
            send_sem=rs_ssem.at[side, k],
            recv_sem=rs_rsem.at[side, k],
            device_id={"dp": sides[side][0]},
            device_id_type=MESH,
        )

    for k in range(7):
        for side in range(2):
            h, hops = sides[side][1][k]
            c = lax.rem(x + hops * sides[side][2], RING)
            value = own(c, h)
            if k >= 2:
                rs_copy(side, k - 2).wait_recv()
                value = value + rs_recv[side, k - 2].astype(F32)
            rs_send[side, k] = value.astype(BF16)
            rs_copy(side, k).start()
        if k == 1:

            def weight_grad(i, carry):
                at = pl.ds(pl.multiple_of(i * 256, 256), 256)
                gd[:, at] = lax.dot_general(
                    received[...],
                    hidden[:, at],
                    (((0,), (0,)), ((), ())),
                    preferred_element_type=F32,
                )
                return carry

            lax.fori_loop(0, ff // 256, weight_grad, 0)

    def z_copy(h):
        return pltpu.make_async_remote_copy(
            src_ref=z_send.at[h],
            dst_ref=z_recv.at[h],
            send_sem=z_sem.at[0, h],
            recv_sem=z_sem.at[1, h],
            device_id={"dp": other},
            device_id_type=MESH,
        )

    for h in (1, 0):
        total = own(x, h)
        for side in range(2):
            k = sides[side][1].index((h, 1))
            rs_copy(side, k).wait_recv()
            total = total + rs_recv[side, k].astype(F32)
        acc[h] = total
        z_send[h] = total.astype(BF16)
        z_copy(h).start()

    ways = ((right, GATHER_RIGHT, RING - 1), (left, GATHER_LEFT, 1))

    def ag_copy(side, h, hops):
        k = ways[side][1].index((h, hops))
        c = lax.rem(x + (hops - 1) * ways[side][2], RING)
        return pltpu.make_async_remote_copy(
            src_ref=grads.at[c, h],
            dst_ref=grads.at[c, h],
            send_sem=ag_ssem.at[side, k],
            recv_sem=ag_rsem.at[side, k],
            device_id={"dp": ways[side][0]},
            device_id_type=MESH,
        )

    for h in (1, 0):
        z_copy(h).wait_recv()
        grads[x, h] = (acc[h] + z_recv[h].astype(F32)).astype(BF16)
        for side in range(2):
            ag_copy(side, h, 1).start()

    loads[2].wait()
    loads[3].wait()

    def finish(chunks):
        d_gate, d_up = [], []
        for c in chunks:
            at = pl.ds(pl.multiple_of(c * chunk, chunk), chunk)
            g = jnp.concatenate([grads[c, 0], grads[c, 1]], axis=1).astype(F32)
            d_gate.append((g * c_gate[at, :]).astype(BF16))
            d_up.append((g * c_up[at, :]).astype(BF16))
        if len(chunks) > 1:
            d_gate, d_up = [jnp.concatenate(d_gate, axis=0)], [jnp.concatenate(d_up, axis=0)]
        across = (((1,), (1,)), ((), ()))
        out = lax.dot_general(d_gate[0], w_gate[...], across, preferred_element_type=F32)
        out = out + lax.dot_general(d_up[0], w_up[...], across, preferred_element_type=F32)
        for n, c in enumerate(chunks):
            mine = out[n * chunk : (n + 1) * chunk]
            first = c * per_chunk
            back_send[pl.ds(first, per_chunk)] = jnp.concatenate(
                [
                    mine[:, :128].reshape(per_chunk, CAP, 128),
                    mine[:, 128:].reshape(per_chunk, CAP, 128),
                ],
                axis=1,
            ).astype(BF16)

            def give_back(i, carry):
                to = first + i

                @pl.when(to != me)
                def _():
                    pltpu.make_async_remote_copy(
                        src_ref=back_send.at[to],
                        dst_ref=back_recv.at[me],
                        send_sem=back_sem.at[0],
                        recv_sem=back_sem.at[1],
                        device_id={"expert": to},
                        device_id_type=MESH,
                    ).start()

                return carry

            lax.fori_loop(0, per_chunk, give_back, 0)

    finish([x])
    for hops in range(1, RING // 2 + 1):
        for n in range(2):
            for side in range(2):
                h = n if side == 0 else 1 - n
                if (h, hops) in ways[side][1]:
                    ag_copy(side, h, hops).wait_recv()
                    if (h, hops + 1) in ways[side][1]:
                        ag_copy(side, h, hops + 1).start()
        if hops < RING // 2:
            finish([lax.rem(x + RING - hops, RING), lax.rem(x + hops, RING)])
        else:
            finish([lax.rem(x + hops, RING)])

    back_recv[pl.ds(me, 1)] = back_send[pl.ds(me, 1)]
    returned = all_but_one(back_send, back_recv, back_sem)
    returned.wait_recv()
    got = back_recv[...].astype(F32)
    table = jnp.concatenate(
        [got[:, :CAP].reshape(slots, 128), got[:, CAP:].reshape(slots, 128)], axis=1
    ).astype(BF16)
    gi[...] = lax.dot_general(
        pick[...], table, (((0,), (0,)), ((), ())), preferred_element_type=F32
    ).astype(BF16)

    arrived.wait_send()
    returned.wait_send()
    for side in range(2):
        for k in range(7):
            rs_copy(side, k).wait_send()
        for h, hops in ways[side][1]:
            ag_copy(side, h, hops).wait_send()
    for h in range(2):
        z_copy(h).wait_send()


def hand_over(gi_in, gd_in, gi_out, gd_out, sem):
    cuts = sem.shape[0] - 1
    tall = gd_in.shape[0] // cuts
    copies = [pltpu.make_async_copy(gi_in, gi_out, sem.at[cuts])]
    for k in range(cuts):
        at = pl.ds(k * tall, tall)
        copies.append(pltpu.make_async_copy(gd_in.at[at], gd_out.at[at], sem.at[k]))
    for copy in copies:
        copy.start()
    for copy in copies:
        copy.wait()


def per_device(dy_values, dy_scales, expert_ids, saved_pre, w_gate, w_up, w_down):
    rows, feats = dy_values.shape
    slots = saved_pre.shape[0]
    ff = w_down.shape[2]
    experts = slots // CAP
    chunk = slots // RING
    vmem = pl.BlockSpec(memory_space=pltpu.VMEM)
    anywhere = pl.BlockSpec(memory_space=pl.ANY)
    shapes = (
        jax.ShapeDtypeStruct((rows, feats), BF16),
        jax.ShapeDtypeStruct((feats, ff), F32),
    )
    results = pl.pallas_call(
        kernel,
        out_shape=tuple(pltpu.VMEM(shape.shape, shape.dtype) for shape in shapes),
        in_specs=[vmem] * 3 + [anywhere] * 4,
        out_specs=(vmem, vmem),
        scratch_shapes=[
            pltpu.VMEM((slots, 2 * ff), BF16),
            pltpu.VMEM((feats, ff), BF16),
            pltpu.VMEM((feats, ff), BF16),
            pltpu.VMEM((feats, ff), BF16),
            pltpu.VMEM((slots, rows), BF16),
            pltpu.VMEM((experts, 2 * CAP, 128), BF16),
            pltpu.VMEM((experts, 2 * CAP, 128), BF16),
            pltpu.VMEM((slots, feats), BF16),
            pltpu.VMEM((slots, ff), BF16),
            pltpu.VMEM((slots, ff), F32),
            pltpu.VMEM((slots, ff), F32),
            pltpu.VMEM((slots, ff), F32),
            pltpu.VMEM((2, 7, chunk, ff // 2), BF16),
            pltpu.VMEM((2, 7, chunk, ff // 2), BF16),
            pltpu.VMEM((2, chunk, ff // 2), F32),
            pltpu.VMEM((2, chunk, ff // 2), BF16),
            pltpu.VMEM((2, chunk, ff // 2), BF16),
            pltpu.VMEM((RING, 2, chunk, ff // 2), BF16),
            pltpu.VMEM((experts, 2 * CAP, 128), BF16),
            pltpu.VMEM((experts, 2 * CAP, 128), BF16),
            pltpu.SemaphoreType.DMA((4,)),
            pltpu.SemaphoreType.DMA((2,)),
            pltpu.SemaphoreType.DMA((2, 7)),
            pltpu.SemaphoreType.DMA((2, 7)),
            pltpu.SemaphoreType.DMA((2, 2)),
            pltpu.SemaphoreType.DMA((2, 7)),
            pltpu.SemaphoreType.DMA((2, 7)),
            pltpu.SemaphoreType.DMA((2,)),
        ],
        compiler_params=pltpu.CompilerParams(
            collective_id=0, has_side_effects=True, vmem_limit_bytes=60 * 1024 * 1024
        ),
        name="experts_backward",
    )(
        expert_ids.reshape(1, rows),
        dy_values,
        dy_scales.T,
        saved_pre,
        w_gate[0],
        w_up[0],
        w_down[0],
    )
    grad_input, grad_down = pl.pallas_call(
        hand_over,
        out_shape=shapes,
        in_specs=[vmem, vmem],
        out_specs=(anywhere, anywhere),
        scratch_shapes=[pltpu.SemaphoreType.DMA((5,))],
        compiler_params=pltpu.CompilerParams(vmem_limit_bytes=4 * 1024 * 1024),
        name="hand_over",
    )(*results)
    return grad_input, grad_down[None]


def solution(mesh):
    return jax.shard_map(
        per_device,
        mesh=mesh,
        in_specs=(
            P("expert", "dp"),
            P("expert", "dp"),
            P("expert", None),
            P("expert", None),
            P("expert", "dp", None),
            P("expert", "dp", None),
            P("expert", "dp", None),
        ),
        out_specs=(P("expert", "dp"), P("expert", "dp", None)),
        check_vma=False,
    )
```

```python
import jax
import jax.numpy as jnp
from jax import lax
from jax.experimental import pallas as pl
from jax.experimental.pallas import tpu as pltpu
from jax.sharding import PartitionSpec as P

MESH = pl.DeviceIdType.MESH
F32, BF16 = jnp.float32, jnp.bfloat16

RING = 8
CAP = 8
Z_HI, Y, CORES = 4, 8, 2

REDUCE_RIGHT = ((0, 4), (1, 3), (0, 3), (1, 2), (0, 2), (1, 1), (0, 1))
REDUCE_LEFT = ((1, 4), (0, 3), (1, 3), (0, 2), (1, 2), (0, 1), (1, 1))
GATHER_RIGHT = ((0, 1), (1, 1), (0, 2), (1, 2), (0, 3), (1, 3), (0, 4))
GATHER_LEFT = ((1, 1), (0, 1), (1, 2), (0, 2), (1, 3), (0, 3), (1, 4))


def kernel(
    ids_ref,
    dy_ref,
    scale_ref,
    saved_hbm,
    gate_hbm,
    up_hbm,
    down_hbm,
    gi,
    gd,
    saved,
    w_gate,
    w_up,
    w_down,
    pick,
    send,
    recv,
    received,
    hidden,
    c_gate,
    c_up,
    part,
    rs_send,
    rs_recv,
    acc,
    z_send,
    z_recv,
    grads,
    back_send,
    back_recv,
    in_sem,
    a2a_sem,
    rs_ssem,
    rs_rsem,
    z_sem,
    ag_ssem,
    ag_rsem,
    back_sem,
):
    experts = send.shape[0]
    slots, feats = received.shape
    ff = hidden.shape[1]
    half_ff = ff // 2
    chunk = slots // RING
    per_chunk = chunk // CAP
    rows = dy_ref.shape[0]

    me = lax.axis_index("expert")
    dp = lax.axis_index("dp")
    x = lax.rem(dp, RING)
    base = dp - x
    right = base + lax.rem(x + 1, RING)
    left = base + lax.rem(x + RING - 1, RING)
    other = lax.rem(dp + RING, 2 * RING)

    loads = [
        pltpu.make_async_copy(src, dst, in_sem.at[k])
        for k, (src, dst) in enumerate(
            ((saved_hbm, saved), (down_hbm, w_down), (gate_hbm, w_gate), (up_hbm, w_up))
        )
    ]
    for load in loads:
        load.start()

    barrier = pltpu.get_barrier_semaphore()

    def centred(k, size):
        step = (k + 1) // 2
        return size // 2 + step - 2 * step * lax.rem(k, 2)

    def nth(k):
        core = lax.rem(me + 1 + k, CORES)
        y = lax.rem(me // CORES + centred(k // CORES % Y, Y), Y)
        z = lax.rem(me // (CORES * Y) + centred(k // (CORES * Y), Z_HI), Z_HI)
        return (z * Y + y) * CORES + core

    def greet(i, carry):
        pl.semaphore_signal(barrier, inc=1, device_id={"expert": nth(i)}, device_id_type=MESH)
        return carry

    lax.fori_loop(0, experts - 1, greet, 0)
    for peer in (right, left, other):
        pl.semaphore_signal(barrier, inc=1, device_id={"dp": peer}, device_id_type=MESH)

    ids = ids_ref[...]
    named = jnp.where(lax.broadcasted_iota(jnp.int32, (experts, rows), 0) == ids, 1.0, 0.0)
    before = jnp.where(
        lax.broadcasted_iota(jnp.int32, (rows, rows), 0)
        < lax.broadcasted_iota(jnp.int32, (rows, rows), 1),
        1.0,
        0.0,
    ).astype(BF16)
    earlier = jnp.dot(named.astype(BF16), before, preferred_element_type=F32)
    rank = jnp.sum(earlier * named, axis=0, keepdims=True)
    position = ids * CAP + rank.astype(jnp.int32)
    hit = lax.broadcasted_iota(jnp.int32, (slots, rows), 0) == position
    pick[...] = jnp.where(hit, 1.0, 0.0).astype(BF16)
    halves = []
    for h in range(2):
        scaled = jnp.where(hit, scale_ref[h : h + 1, :].astype(F32), 0.0).astype(BF16)
        rows_h = jnp.dot(
            scaled, dy_ref[:, h * 128 : (h + 1) * 128], preferred_element_type=F32
        )
        halves.append(rows_h.reshape(experts, CAP, 128))
    send[...] = jnp.concatenate(halves, axis=1).astype(BF16)

    pl.semaphore_wait(barrier, experts - 1 + 3)

    def dispatch(i, carry):
        to = nth(i)
        pltpu.make_async_remote_copy(
            src_ref=send.at[to],
            dst_ref=recv.at[me],
            send_sem=a2a_sem.at[0],
            recv_sem=a2a_sem.at[1],
            device_id={"expert": to},
            device_id_type=MESH,
        ).start()
        return carry

    lax.fori_loop(0, experts - 1, dispatch, 0)
    recv[pl.ds(me, 1)] = send[pl.ds(me, 1)]

    loads[0].wait()
    step = 16

    def activate(i, carry):
        at = pl.ds(pl.multiple_of(i * step, step), step)
        gate = saved[at, :ff].astype(F32)
        up = saved[at, ff:].astype(F32)
        sig = jax.nn.sigmoid(gate)
        silu = gate * sig
        c_up[at, :] = silu
        c_gate[at, :] = up * sig * (1.0 + gate * (1.0 - sig))
        hidden[at, :] = (silu * up).astype(BF16)
        return carry

    lax.fori_loop(0, slots // step, activate, 0)

    def all_but_one(buf_a, buf_b, sems):
        n = pl.ds(0, experts - 1)
        return pltpu.make_async_remote_copy(
            src_ref=buf_a.at[n],
            dst_ref=buf_b.at[n],
            send_sem=sems.at[0],
            recv_sem=sems.at[1],
            device_id={"expert": lax.rem(me + 1, experts)},
            device_id_type=MESH,
        )

    arrived = all_but_one(send, recv, a2a_sem)
    arrived.wait_recv()
    got = recv[...].astype(F32)
    received[...] = jnp.concatenate(
        [got[:, :CAP].reshape(slots, 128), got[:, CAP:].reshape(slots, 128)], axis=1
    ).astype(BF16)

    loads[1].wait()
    block = 128

    def project(i, carry):
        at = pl.ds(pl.multiple_of(i * block, block), block)
        part[at, :] = jnp.dot(received[at, :], w_down[...], preferred_element_type=F32)
        return carry

    lax.fori_loop(0, slots // block, project, 0)

    def own(c, h):
        at = pl.ds(pl.multiple_of(c * chunk, chunk), chunk)
        return part[at, h * half_ff : (h + 1) * half_ff]

    sides = ((right, REDUCE_RIGHT, 1), (left, REDUCE_LEFT, RING - 1))

    def rs_copy(side, k):
        return pltpu.make_async_remote_copy(
            src_ref=rs_send.at[side, k],
            dst_ref=rs_recv.at[side, k],
            send_sem=rs_ssem.at[side, k],
            recv_sem=rs_rsem.at[side, k],
            device_id={"dp": sides[side][0]},
            device_id_type=MESH,
        )

    for k in range(7):
        for side in range(2):
            h, hops = sides[side][1][k]
            c = lax.rem(x + hops * sides[side][2], RING)
            value = own(c, h)
            if k >= 2:
                rs_copy(side, k - 2).wait_recv()
                value = value + rs_recv[side, k - 2].astype(F32)
            rs_send[side, k] = value.astype(BF16)
            rs_copy(side, k).start()
        if k == 1:

            def weight_grad(i, carry):
                at = pl.ds(pl.multiple_of(i * 256, 256), 256)
                gd[:, at] = lax.dot_general(
                    received[...],
                    hidden[:, at],
                    (((0,), (0,)), ((), ())),
                    preferred_element_type=F32,
                )
                return carry

            lax.fori_loop(0, ff // 256, weight_grad, 0)

    def z_copy(h):
        return pltpu.make_async_remote_copy(
            src_ref=z_send.at[h],
            dst_ref=z_recv.at[h],
            send_sem=z_sem.at[0, h],
            recv_sem=z_sem.at[1, h],
            device_id={"dp": other},
            device_id_type=MESH,
        )

    for h in (1, 0):
        total = own(x, h)
        for side in range(2):
            k = sides[side][1].index((h, 1))
            rs_copy(side, k).wait_recv()
            total = total + rs_recv[side, k].astype(F32)
        acc[h] = total
        z_send[h] = total.astype(BF16)
        z_copy(h).start()

    ways = ((right, GATHER_RIGHT, RING - 1), (left, GATHER_LEFT, 1))

    def ag_copy(side, h, hops):
        k = ways[side][1].index((h, hops))
        c = lax.rem(x + (hops - 1) * ways[side][2], RING)
        return pltpu.make_async_remote_copy(
            src_ref=grads.at[c, h],
            dst_ref=grads.at[c, h],
            send_sem=ag_ssem.at[side, k],
            recv_sem=ag_rsem.at[side, k],
            device_id={"dp": ways[side][0]},
            device_id_type=MESH,
        )

    for h in (1, 0):
        z_copy(h).wait_recv()
        grads[x, h] = (acc[h] + z_recv[h].astype(F32)).astype(BF16)
        for side in range(2):
            ag_copy(side, h, 1).start()

    loads[2].wait()
    loads[3].wait()

    def finish(chunks):
        d_gate, d_up = [], []
        for c in chunks:
            at = pl.ds(pl.multiple_of(c * chunk, chunk), chunk)
            g = jnp.concatenate([grads[c, 0], grads[c, 1]], axis=1).astype(F32)
            d_gate.append((g * c_gate[at, :]).astype(BF16))
            d_up.append((g * c_up[at, :]).astype(BF16))
        if len(chunks) > 1:
            d_gate, d_up = [jnp.concatenate(d_gate, axis=0)], [jnp.concatenate(d_up, axis=0)]
        across = (((1,), (1,)), ((), ()))
        out = lax.dot_general(d_gate[0], w_gate[...], across, preferred_element_type=F32)
        out = out + lax.dot_general(d_up[0], w_up[...], across, preferred_element_type=F32)
        for n, c in enumerate(chunks):
            mine = out[n * chunk : (n + 1) * chunk]
            first = c * per_chunk
            back_send[pl.ds(first, per_chunk)] = jnp.concatenate(
                [
                    mine[:, :128].reshape(per_chunk, CAP, 128),
                    mine[:, 128:].reshape(per_chunk, CAP, 128),
                ],
                axis=1,
            ).astype(BF16)

            def give_back(i, carry):
                to = first + i

                @pl.when(to != me)
                def _():
                    pltpu.make_async_remote_copy(
                        src_ref=back_send.at[to],
                        dst_ref=back_recv.at[me],
                        send_sem=back_sem.at[0],
                        recv_sem=back_sem.at[1],
                        device_id={"expert": to},
                        device_id_type=MESH,
                    ).start()

                return carry

            lax.fori_loop(0, per_chunk, give_back, 0)

    finish([x])
    for hops in range(1, RING // 2 + 1):
        for n in range(2):
            for side in range(2):
                h = n if side == 0 else 1 - n
                if (h, hops) in ways[side][1]:
                    ag_copy(side, h, hops).wait_recv()
                    if (h, hops + 1) in ways[side][1]:
                        ag_copy(side, h, hops + 1).start()
        if hops < RING // 2:
            finish([lax.rem(x + RING - hops, RING), lax.rem(x + hops, RING)])
        else:
            finish([lax.rem(x + hops, RING)])

    back_recv[pl.ds(me, 1)] = back_send[pl.ds(me, 1)]
    returned = all_but_one(back_send, back_recv, back_sem)
    returned.wait_recv()
    got = back_recv[...].astype(F32)
    table = jnp.concatenate(
        [got[:, :CAP].reshape(slots, 128), got[:, CAP:].reshape(slots, 128)], axis=1
    ).astype(BF16)
    gi[...] = lax.dot_general(
        pick[...], table, (((0,), (0,)), ((), ())), preferred_element_type=F32
    ).astype(BF16)

    arrived.wait_send()
    returned.wait_send()
    for side in range(2):
        for k in range(7):
            rs_copy(side, k).wait_send()
        for h, hops in ways[side][1]:
            ag_copy(side, h, hops).wait_send()
    for h in range(2):
        z_copy(h).wait_send()


def hand_over(gi_in, gd_in, gi_out, gd_out, sem):
    cuts = sem.shape[0] - 1
    tall = gd_in.shape[0] // cuts
    copies = [pltpu.make_async_copy(gi_in, gi_out, sem.at[cuts])]
    for k in range(cuts):
        at = pl.ds(k * tall, tall)
        copies.append(pltpu.make_async_copy(gd_in.at[at], gd_out.at[at], sem.at[k]))
    for copy in copies:
        copy.start()
    for copy in copies:
        copy.wait()


def per_device(dy_values, dy_scales, expert_ids, saved_pre, w_gate, w_up, w_down):
    rows, feats = dy_values.shape
    slots = saved_pre.shape[0]
    ff = w_down.shape[2]
    experts = slots // CAP
    chunk = slots // RING
    vmem = pl.BlockSpec(memory_space=pltpu.VMEM)
    anywhere = pl.BlockSpec(memory_space=pl.ANY)
    shapes = (
        jax.ShapeDtypeStruct((rows, feats), BF16),
        jax.ShapeDtypeStruct((feats, ff), F32),
    )
    results = pl.pallas_call(
        kernel,
        out_shape=tuple(pltpu.VMEM(shape.shape, shape.dtype) for shape in shapes),
        in_specs=[vmem] * 3 + [anywhere] * 4,
        out_specs=(vmem, vmem),
        scratch_shapes=[
            pltpu.VMEM((slots, 2 * ff), BF16),
            pltpu.VMEM((feats, ff), BF16),
            pltpu.VMEM((feats, ff), BF16),
            pltpu.VMEM((feats, ff), BF16),
            pltpu.VMEM((slots, rows), BF16),
            pltpu.VMEM((experts, 2 * CAP, 128), BF16),
            pltpu.VMEM((experts, 2 * CAP, 128), BF16),
            pltpu.VMEM((slots, feats), BF16),
            pltpu.VMEM((slots, ff), BF16),
            pltpu.VMEM((slots, ff), F32),
            pltpu.VMEM((slots, ff), F32),
            pltpu.VMEM((slots, ff), F32),
            pltpu.VMEM((2, 7, chunk, ff // 2), BF16),
            pltpu.VMEM((2, 7, chunk, ff // 2), BF16),
            pltpu.VMEM((2, chunk, ff // 2), F32),
            pltpu.VMEM((2, chunk, ff // 2), BF16),
            pltpu.VMEM((2, chunk, ff // 2), BF16),
            pltpu.VMEM((RING, 2, chunk, ff // 2), BF16),
            pltpu.VMEM((experts, 2 * CAP, 128), BF16),
            pltpu.VMEM((experts, 2 * CAP, 128), BF16),
            pltpu.SemaphoreType.DMA((4,)),
            pltpu.SemaphoreType.DMA((2,)),
            pltpu.SemaphoreType.DMA((2, 7)),
            pltpu.SemaphoreType.DMA((2, 7)),
            pltpu.SemaphoreType.DMA((2, 2)),
            pltpu.SemaphoreType.DMA((2, 7)),
            pltpu.SemaphoreType.DMA((2, 7)),
            pltpu.SemaphoreType.DMA((2,)),
        ],
        compiler_params=pltpu.CompilerParams(
            collective_id=0, has_side_effects=True, vmem_limit_bytes=60 * 1024 * 1024
        ),
        name="experts_backward",
    )(
        expert_ids.reshape(1, rows),
        dy_values,
        dy_scales.T,
        saved_pre,
        w_gate[0],
        w_up[0],
        w_down[0],
    )
    grad_input, grad_down = pl.pallas_call(
        hand_over,
        out_shape=shapes,
        in_specs=[vmem, vmem],
        out_specs=(anywhere, anywhere),
        scratch_shapes=[pltpu.SemaphoreType.DMA((5,))],
        compiler_params=pltpu.CompilerParams(vmem_limit_bytes=4 * 1024 * 1024),
        name="hand_over",
    )(*results)
    return grad_input, grad_down[None]


def solution(mesh):
    return jax.shard_map(
        per_device,
        mesh=mesh,
        in_specs=(
            P("expert", "dp"),
            P("expert", "dp"),
            P("expert", None),
            P("expert", None),
            P("expert", "dp", None),
            P("expert", "dp", None),
            P("expert", "dp", None),
        ),
        out_specs=(P("expert", "dp"), P("expert", "dp", None)),
        check_vma=False,
    )
```

```python
import jax
import jax.numpy as jnp
from jax import lax
from jax.experimental import pallas as pl
from jax.experimental.pallas import tpu as pltpu
from jax.sharding import PartitionSpec as P

MESH = pl.DeviceIdType.MESH
F32, BF16 = jnp.float32, jnp.bfloat16

RING = 8
CAP = 8
Z_HI, Y, CORES = 4, 8, 2

REDUCE_RIGHT = ((0, 4), (1, 3), (0, 3), (1, 2), (0, 2), (1, 1), (0, 1))
REDUCE_LEFT = ((1, 4), (0, 3), (1, 3), (0, 2), (1, 2), (0, 1), (1, 1))
GATHER_RIGHT = ((0, 1), (1, 1), (0, 2), (1, 2), (0, 3), (1, 3), (0, 4))
GATHER_LEFT = ((1, 1), (0, 1), (1, 2), (0, 2), (1, 3), (0, 3), (1, 4))


def kernel(
    ids_ref,
    dy_ref,
    scale_ref,
    saved_hbm,
    gate_hbm,
    up_hbm,
    down_hbm,
    gi,
    gd,
    saved,
    w_gate,
    w_up,
    w_down,
    pick,
    send,
    recv,
    received,
    hidden,
    c_gate,
    c_up,
    part,
    rs_send,
    rs_recv,
    acc,
    z_send,
    z_recv,
    grads,
    back_send,
    back_recv,
    in_sem,
    a2a_sem,
    rs_ssem,
    rs_rsem,
    z_sem,
    ag_ssem,
    ag_rsem,
    back_sem,
):
    experts = send.shape[0]
    slots, feats = received.shape
    ff = hidden.shape[1]
    half_ff = ff // 2
    chunk = slots // RING
    per_chunk = chunk // CAP
    rows = dy_ref.shape[0]

    me = lax.axis_index("expert")
    dp = lax.axis_index("dp")
    x = lax.rem(dp, RING)
    base = dp - x
    right = base + lax.rem(x + 1, RING)
    left = base + lax.rem(x + RING - 1, RING)
    other = lax.rem(dp + RING, 2 * RING)

    loads = [
        pltpu.make_async_copy(src, dst, in_sem.at[k])
        for k, (src, dst) in enumerate(
            ((saved_hbm, saved), (down_hbm, w_down), (gate_hbm, w_gate), (up_hbm, w_up))
        )
    ]
    for load in loads:
        load.start()

    barrier = pltpu.get_barrier_semaphore()

    def centred(k, size):
        step = (k + 1) // 2
        return size // 2 + (step - 2 * step * lax.rem(k, 2)) * (1 - 2 * lax.rem(me, CORES))

    def nth(k):
        core = lax.rem(me + 1 + k, CORES)
        y = lax.rem(me // CORES + centred(k // CORES % Y, Y), Y)
        z = lax.rem(me // (CORES * Y) + centred(k // (CORES * Y), Z_HI), Z_HI)
        return (z * Y + y) * CORES + core

    def greet(i, carry):
        pl.semaphore_signal(barrier, inc=1, device_id={"expert": nth(i)}, device_id_type=MESH)
        return carry

    lax.fori_loop(0, experts - 1, greet, 0)
    for peer in (right, left, other):
        pl.semaphore_signal(barrier, inc=1, device_id={"dp": peer}, device_id_type=MESH)

    ids = ids_ref[...]
    named = jnp.where(lax.broadcasted_iota(jnp.int32, (experts, rows), 0) == ids, 1.0, 0.0)
    before = jnp.where(
        lax.broadcasted_iota(jnp.int32, (rows, rows), 0)
        < lax.broadcasted_iota(jnp.int32, (rows, rows), 1),
        1.0,
        0.0,
    ).astype(BF16)
    earlier = jnp.dot(named.astype(BF16), before, preferred_element_type=F32)
    rank = jnp.sum(earlier * named, axis=0, keepdims=True)
    position = ids * CAP + rank.astype(jnp.int32)
    hit = lax.broadcasted_iota(jnp.int32, (slots, rows), 0) == position
    pick[...] = jnp.where(hit, 1.0, 0.0).astype(BF16)
    halves = []
    for h in range(2):
        scaled = jnp.where(hit, scale_ref[h : h + 1, :].astype(F32), 0.0).astype(BF16)
        rows_h = jnp.dot(
            scaled, dy_ref[:, h * 128 : (h + 1) * 128], preferred_element_type=F32
        )
        halves.append(rows_h.reshape(experts, CAP, 128))
    send[...] = jnp.concatenate(halves, axis=1).astype(BF16)

    pl.semaphore_wait(barrier, experts - 1 + 3)

    def dispatch(i, carry):
        to = nth(i)
        pltpu.make_async_remote_copy(
            src_ref=send.at[to],
            dst_ref=recv.at[me],
            send_sem=a2a_sem.at[0],
            recv_sem=a2a_sem.at[1],
            device_id={"expert": to},
            device_id_type=MESH,
        ).start()
        return carry

    lax.fori_loop(0, experts - 1, dispatch, 0)
    recv[pl.ds(me, 1)] = send[pl.ds(me, 1)]

    loads[0].wait()
    step = 16

    def activate(i, carry):
        at = pl.ds(pl.multiple_of(i * step, step), step)
        gate = saved[at, :ff].astype(F32)
        up = saved[at, ff:].astype(F32)
        sig = jax.nn.sigmoid(gate)
        silu = gate * sig
        c_up[at, :] = silu
        c_gate[at, :] = up * sig * (1.0 + gate * (1.0 - sig))
        hidden[at, :] = (silu * up).astype(BF16)
        return carry

    lax.fori_loop(0, slots // step, activate, 0)

    def all_but_one(buf_a, buf_b, sems):
        n = pl.ds(0, experts - 1)
        return pltpu.make_async_remote_copy(
            src_ref=buf_a.at[n],
            dst_ref=buf_b.at[n],
            send_sem=sems.at[0],
            recv_sem=sems.at[1],
            device_id={"expert": lax.rem(me + 1, experts)},
            device_id_type=MESH,
        )

    arrived = all_but_one(send, recv, a2a_sem)
    arrived.wait_recv()
    got = recv[...].astype(F32)
    received[...] = jnp.concatenate(
        [got[:, :CAP].reshape(slots, 128), got[:, CAP:].reshape(slots, 128)], axis=1
    ).astype(BF16)

    loads[1].wait()
    block = 128

    def project(i, carry):
        at = pl.ds(pl.multiple_of(i * block, block), block)
        part[at, :] = jnp.dot(received[at, :], w_down[...], preferred_element_type=F32)
        return carry

    lax.fori_loop(0, slots // block, project, 0)

    def own(c, h):
        at = pl.ds(pl.multiple_of(c * chunk, chunk), chunk)
        return part[at, h * half_ff : (h + 1) * half_ff]

    sides = ((right, REDUCE_RIGHT, 1), (left, REDUCE_LEFT, RING - 1))

    def rs_copy(side, k):
        return pltpu.make_async_remote_copy(
            src_ref=rs_send.at[side, k],
            dst_ref=rs_recv.at[side, k],
            send_sem=rs_ssem.at[side, k],
            recv_sem=rs_rsem.at[side, k],
            device_id={"dp": sides[side][0]},
            device_id_type=MESH,
        )

    for k in range(7):
        for side in range(2):
            h, hops = sides[side][1][k]
            c = lax.rem(x + hops * sides[side][2], RING)
            value = own(c, h)
            if k >= 2:
                rs_copy(side, k - 2).wait_recv()
                value = value + rs_recv[side, k - 2].astype(F32)
            rs_send[side, k] = value.astype(BF16)
            rs_copy(side, k).start()
        if k == 1:

            def weight_grad(i, carry):
                at = pl.ds(pl.multiple_of(i * 256, 256), 256)
                gd[:, at] = lax.dot_general(
                    received[...],
                    hidden[:, at],
                    (((0,), (0,)), ((), ())),
                    preferred_element_type=F32,
                )
                return carry

            lax.fori_loop(0, ff // 256, weight_grad, 0)

    def z_copy(h):
        return pltpu.make_async_remote_copy(
            src_ref=z_send.at[h],
            dst_ref=z_recv.at[h],
            send_sem=z_sem.at[0, h],
            recv_sem=z_sem.at[1, h],
            device_id={"dp": other},
            device_id_type=MESH,
        )

    for h in (1, 0):
        total = own(x, h)
        for side in range(2):
            k = sides[side][1].index((h, 1))
            rs_copy(side, k).wait_recv()
            total = total + rs_recv[side, k].astype(F32)
        acc[h] = total
        z_send[h] = total.astype(BF16)
        z_copy(h).start()

    ways = ((right, GATHER_RIGHT, RING - 1), (left, GATHER_LEFT, 1))

    def ag_copy(side, h, hops):
        k = ways[side][1].index((h, hops))
        c = lax.rem(x + (hops - 1) * ways[side][2], RING)
        return pltpu.make_async_remote_copy(
            src_ref=grads.at[c, h],
            dst_ref=grads.at[c, h],
            send_sem=ag_ssem.at[side, k],
            recv_sem=ag_rsem.at[side, k],
            device_id={"dp": ways[side][0]},
            device_id_type=MESH,
        )

    for h in (1, 0):
        z_copy(h).wait_recv()
        grads[x, h] = (acc[h] + z_recv[h].astype(F32)).astype(BF16)
        for side in range(2):
            ag_copy(side, h, 1).start()

    loads[2].wait()
    loads[3].wait()

    def finish(chunks):
        d_gate, d_up = [], []
        for c in chunks:
            at = pl.ds(pl.multiple_of(c * chunk, chunk), chunk)
            g = jnp.concatenate([grads[c, 0], grads[c, 1]], axis=1).astype(F32)
            d_gate.append((g * c_gate[at, :]).astype(BF16))
            d_up.append((g * c_up[at, :]).astype(BF16))
        if len(chunks) > 1:
            d_gate, d_up = [jnp.concatenate(d_gate, axis=0)], [jnp.concatenate(d_up, axis=0)]
        across = (((1,), (1,)), ((), ()))
        out = lax.dot_general(d_gate[0], w_gate[...], across, preferred_element_type=F32)
        out = out + lax.dot_general(d_up[0], w_up[...], across, preferred_element_type=F32)
        for n, c in enumerate(chunks):
            mine = out[n * chunk : (n + 1) * chunk]
            first = c * per_chunk
            back_send[pl.ds(first, per_chunk)] = jnp.concatenate(
                [
                    mine[:, :128].reshape(per_chunk, CAP, 128),
                    mine[:, 128:].reshape(per_chunk, CAP, 128),
                ],
                axis=1,
            ).astype(BF16)

            def give_back(i, carry):
                to = first + i

                @pl.when(to != me)
                def _():
                    pltpu.make_async_remote_copy(
                        src_ref=back_send.at[to],
                        dst_ref=back_recv.at[me],
                        send_sem=back_sem.at[0],
                        recv_sem=back_sem.at[1],
                        device_id={"expert": to},
                        device_id_type=MESH,
                    ).start()

                return carry

            lax.fori_loop(0, per_chunk, give_back, 0)

    finish([x])
    for hops in range(1, RING // 2 + 1):
        for n in range(2):
            for side in range(2):
                h = n if side == 0 else 1 - n
                if (h, hops) in ways[side][1]:
                    ag_copy(side, h, hops).wait_recv()
                    if (h, hops + 1) in ways[side][1]:
                        ag_copy(side, h, hops + 1).start()
        if hops < RING // 2:
            finish([lax.rem(x + RING - hops, RING), lax.rem(x + hops, RING)])
        else:
            finish([lax.rem(x + hops, RING)])

    back_recv[pl.ds(me, 1)] = back_send[pl.ds(me, 1)]
    returned = all_but_one(back_send, back_recv, back_sem)
    returned.wait_recv()
    got = back_recv[...].astype(F32)
    table = jnp.concatenate(
        [got[:, :CAP].reshape(slots, 128), got[:, CAP:].reshape(slots, 128)], axis=1
    ).astype(BF16)
    gi[...] = lax.dot_general(
        pick[...], table, (((0,), (0,)), ((), ())), preferred_element_type=F32
    ).astype(BF16)

    arrived.wait_send()
    returned.wait_send()
    for side in range(2):
        for k in range(7):
            rs_copy(side, k).wait_send()
        for h, hops in ways[side][1]:
            ag_copy(side, h, hops).wait_send()
    for h in range(2):
        z_copy(h).wait_send()


def hand_over(gi_in, gd_in, gi_out, gd_out, sem):
    cuts = sem.shape[0] - 1
    tall = gd_in.shape[0] // cuts
    copies = [pltpu.make_async_copy(gi_in, gi_out, sem.at[cuts])]
    for k in range(cuts):
        at = pl.ds(k * tall, tall)
        copies.append(pltpu.make_async_copy(gd_in.at[at], gd_out.at[at], sem.at[k]))
    for copy in copies:
        copy.start()
    for copy in copies:
        copy.wait()


def per_device(dy_values, dy_scales, expert_ids, saved_pre, w_gate, w_up, w_down):
    rows, feats = dy_values.shape
    slots = saved_pre.shape[0]
    ff = w_down.shape[2]
    experts = slots // CAP
    chunk = slots // RING
    vmem = pl.BlockSpec(memory_space=pltpu.VMEM)
    anywhere = pl.BlockSpec(memory_space=pl.ANY)
    shapes = (
        jax.ShapeDtypeStruct((rows, feats), BF16),
        jax.ShapeDtypeStruct((feats, ff), F32),
    )
    results = pl.pallas_call(
        kernel,
        out_shape=tuple(pltpu.VMEM(shape.shape, shape.dtype) for shape in shapes),
        in_specs=[vmem] * 3 + [anywhere] * 4,
        out_specs=(vmem, vmem),
        scratch_shapes=[
            pltpu.VMEM((slots, 2 * ff), BF16),
            pltpu.VMEM((feats, ff), BF16),
            pltpu.VMEM((feats, ff), BF16),
            pltpu.VMEM((feats, ff), BF16),
            pltpu.VMEM((slots, rows), BF16),
            pltpu.VMEM((experts, 2 * CAP, 128), BF16),
            pltpu.VMEM((experts, 2 * CAP, 128), BF16),
            pltpu.VMEM((slots, feats), BF16),
            pltpu.VMEM((slots, ff), BF16),
            pltpu.VMEM((slots, ff), F32),
            pltpu.VMEM((slots, ff), F32),
            pltpu.VMEM((slots, ff), F32),
            pltpu.VMEM((2, 7, chunk, ff // 2), BF16),
            pltpu.VMEM((2, 7, chunk, ff // 2), BF16),
            pltpu.VMEM((2, chunk, ff // 2), F32),
            pltpu.VMEM((2, chunk, ff // 2), BF16),
            pltpu.VMEM((2, chunk, ff // 2), BF16),
            pltpu.VMEM((RING, 2, chunk, ff // 2), BF16),
            pltpu.VMEM((experts, 2 * CAP, 128), BF16),
            pltpu.VMEM((experts, 2 * CAP, 128), BF16),
            pltpu.SemaphoreType.DMA((4,)),
            pltpu.SemaphoreType.DMA((2,)),
            pltpu.SemaphoreType.DMA((2, 7)),
            pltpu.SemaphoreType.DMA((2, 7)),
            pltpu.SemaphoreType.DMA((2, 2)),
            pltpu.SemaphoreType.DMA((2, 7)),
            pltpu.SemaphoreType.DMA((2, 7)),
            pltpu.SemaphoreType.DMA((2,)),
        ],
        compiler_params=pltpu.CompilerParams(
            collective_id=0, has_side_effects=True, vmem_limit_bytes=60 * 1024 * 1024
        ),
        name="experts_backward",
    )(
        expert_ids.reshape(1, rows),
        dy_values,
        dy_scales.T,
        saved_pre,
        w_gate[0],
        w_up[0],
        w_down[0],
    )
    grad_input, grad_down = pl.pallas_call(
        hand_over,
        out_shape=shapes,
        in_specs=[vmem, vmem],
        out_specs=(anywhere, anywhere),
        scratch_shapes=[pltpu.SemaphoreType.DMA((5,))],
        compiler_params=pltpu.CompilerParams(vmem_limit_bytes=4 * 1024 * 1024),
        name="hand_over",
    )(*results)
    return grad_input, grad_down[None]


def solution(mesh):
    return jax.shard_map(
        per_device,
        mesh=mesh,
        in_specs=(
            P("expert", "dp"),
            P("expert", "dp"),
            P("expert", None),
            P("expert", None),
            P("expert", "dp", None),
            P("expert", "dp", None),
            P("expert", "dp", None),
        ),
        out_specs=(P("expert", "dp"), P("expert", "dp", None)),
        check_vma=False,
    )
```
